256 devices in a mesh: gx: 16 (over z, x_hi), gy: 16 (over y, x_lo, core).
Axes of the slice: x: 4 (x_hi: 2, x_lo: 2; x = x_hi * 2 + x_lo), y: 4, z: 8, core: 2. Of those that a mesh axis runs over, the one named last changes fastest.
Arguments:
- saturation: bfloat16 [20, 256, 256, 256], P(None, 'gx', 'gy'), may hold values from -6 to 6
- spectral_weight: float32 [2, 768, 24, 20, 20], P(None, ('gx', 'gy')), may hold values from -18 to 18
- pointwise_weight: bfloat16 [20, 20], replicated, may hold values from -1.25 to 1.25
- pointwise_bias: float32 [20], replicated, may hold values from -3 to 3
- cotangent: bfloat16 [20, 256, 256, 256], P(None, 'gx', 'gy'), may hold values from -6 to 6
Outputs:
- layer_output: bfloat16 [20, 256, 256, 256], P(None, 'gx', 'gy')
- input_gradient: bfloat16 [20, 256, 256, 256], P(None, 'gx', 'gy')
- spectral_gradient: float32 [2, 768, 24, 20, 20], P(None, ('gx', 'gy'))
The draws below stay inside these ranges and needn't reach their ends.
All inputs are finite; a program needn't handle non-finite values.
Results may differ from the reference program's by a relative error of at most 0.038.
Values may be sent and summed in bfloat16 or wider, within the bound.
No kernel may reach another device: no remote copies, remote signals or barrier semaphores. Data moves between devices by JAX's collectives and lax.ppermute only.
A program may use at most 128 MiB of HBM per device.

```python
import math
import jax
import jax.numpy as jnp
from jax import lax

C = 20
CX = 16
Z = 32
T_SIZE = 8
KX = 24
KY = 24
KZ = 8
KT = 4
X = 256
Y = 256
ZT = 256
M = 32
MK = 768


def shard_levels(key, dims, split, least, largest):
    def one(dim, shards_of):
        heights = jax.random.uniform(jax.random.fold_in(jax.random.fold_in(key, 6), dim), (shards_of,), jnp.float32, least / len(split), largest / len(split))
        return jnp.repeat(jnp.exp(heights), dims[dim] // shards_of).reshape((-1,) + (1,) * (len(dims) - dim - 1))

    factor_of = one(*split[0])
    for cut in split[1:]:
        factor_of = factor_of * one(*cut)
    return factor_of


def centred(own_key, extent, width, limit, cuts=(), kind=jnp.bfloat16):
    loudness = shard_levels(own_key, extent, cuts, -0.22, 0.18) if cuts else 1.0
    drawn = jax.random.normal(own_key, extent, jnp.float32) * width * loudness
    return jnp.minimum(jnp.maximum(drawn, -limit), limit).astype(kind)


def setup_inputs(seed: int = 0) -> dict:
    seeds = jax.random.split(jax.random.key(seed), 6)
    saturation = centred(seeds[0], (C, X, Y, ZT), 1.0, 6.0, ((1, 16), (2, 16)))
    spectral_weight = centred(seeds[1], (2, MK, KY, C, C), 3.0, 18.0, ((1, 256),), jnp.float32)
    pointwise_weight = centred(seeds[2], (C, C), C ** -0.5, 1.25)
    pointwise_bias = centred(seeds[3], (C,), 0.5, 3.0, (), jnp.float32)
    cotangent = centred(seeds[4], (C, X, Y, ZT), 1.0, 6.0, ((1, 16), (2, 16)))
    return {"saturation": saturation, "spectral_weight": spectral_weight, "pointwise_weight": pointwise_weight, "pointwise_bias": pointwise_bias, "cotangent": cotangent}


highest = lax.Precision.HIGHEST

def kept_frequency(kept_count):
    position = jnp.arange(kept_count, dtype=jnp.int32)
    return jnp.where(position < kept_count // 2, position, position - kept_count)

def axis_table(length, kept_count, offset, row_total):
    positions = offset + jnp.arange(row_total, dtype=jnp.int32)
    product = positions[:, None] * kept_frequency(kept_count)[None, :] % length
    phase_angle = product.astype(jnp.float32) * (2.0 * math.pi / length)
    cosine = jnp.cos(phase_angle) * (1.0 / math.sqrt(length))
    sine_part = jnp.sin(phase_angle) * (1.0 / math.sqrt(length))
    real_rows = jnp.stack([cosine, -sine_part], axis=-1)
    imag_rows = jnp.stack([sine_part, cosine], axis=-1)
    return jnp.stack([real_rows, imag_rows], axis=1).astype(jnp.bfloat16)

def depth_time_table():
    cell_index = jnp.arange(Z * T_SIZE, dtype=jnp.int32)
    depth_index = cell_index // T_SIZE
    time_index = cell_index % T_SIZE
    depth_part = (depth_index[:, None] * kept_frequency(KZ)[None, :] % Z).astype(jnp.float32) * (1.0 / Z)
    time_part = (time_index[:, None] * jnp.arange(KT, dtype=jnp.int32)[None, :] % T_SIZE).astype(jnp.float32) * (1.0 / T_SIZE)
    phase_angle = (depth_part[:, :, None] + time_part[:, None, :]).reshape(Z * T_SIZE, KZ * KT) * (2.0 * math.pi)
    norm_scale = 1.0 / math.sqrt(Z * T_SIZE)
    return jnp.stack([jnp.cos(phase_angle) * norm_scale, -jnp.sin(phase_angle) * norm_scale], axis=-1).astype(jnp.bfloat16)

def gelu_value(pre_value):
    return 0.5 * pre_value * (1.0 + lax.erf(pre_value * (1.0 / math.sqrt(2.0))))

def gelu_slope(pre_value):
    return 0.5 * (1.0 + lax.erf(pre_value * (1.0 / math.sqrt(2.0)))) + pre_value * jnp.exp(-0.5 * pre_value * pre_value) * (1.0 / math.sqrt(2.0 * math.pi))

def mix(spectrum, weight_real, weight_imag):
    real_part = spectrum[:, :, 0, :]
    imag_part = spectrum[:, :, 1, :]
    out_real = jnp.einsum('slio,sli->slo', weight_real, real_part, precision=highest) - jnp.einsum('slio,sli->slo', weight_imag, imag_part, precision=highest)
    out_imag = jnp.einsum('slio,sli->slo', weight_real, imag_part, precision=highest) + jnp.einsum('slio,sli->slo', weight_imag, real_part, precision=highest)
    return jnp.stack([out_real, out_imag], axis=2)

def outer_gradient(spectrum, upstream):
    real_part = spectrum[:, :, 0, :]
    imag_part = spectrum[:, :, 1, :]
    upstream_real = upstream[:, :, 0, :]
    upstream_imag = upstream[:, :, 1, :]
    real_gradient = jnp.einsum('slo,sli->slio', upstream_real, real_part, precision=highest) + jnp.einsum('slo,sli->slio', upstream_imag, imag_part, precision=highest)
    imag_gradient = jnp.einsum('slo,sli->slio', upstream_imag, real_part, precision=highest) - jnp.einsum('slo,sli->slio', upstream_real, imag_part, precision=highest)
    return jnp.stack([real_gradient, imag_gradient], axis=0)

def back_mix(upstream, weight_real, weight_imag):
    upstream_real = upstream[:, :, 0, :]
    upstream_imag = upstream[:, :, 1, :]
    into_real = jnp.einsum('slio,slo->sli', weight_real, upstream_real, precision=highest) + jnp.einsum('slio,slo->sli', weight_imag, upstream_imag, precision=highest)
    into_imag = jnp.einsum('slio,slo->sli', weight_real, upstream_imag, precision=highest) - jnp.einsum('slio,slo->sli', weight_imag, upstream_real, precision=highest)
    return jnp.stack([into_real, into_imag], axis=2)

def mode_factor(item_total):
    item_index = jnp.arange(item_total, dtype=jnp.int32)
    return jnp.where(item_index // KX % KT == 0, 1.0, 2.0).astype(jnp.float32)

def split_blocks(volume):
    return volume.reshape(C, X // CX, CX, Y, ZT).transpose(1, 0, 2, 3, 4)

def join_blocks(blocks):
    return blocks.transpose(1, 0, 2, 3, 4).reshape(C, X, Y, ZT)

def analyse(volume, depth_table, row_table, column_table):
    depth_floats = depth_table.astype(jnp.float32)

    def one_block(row_block):
        return jnp.einsum('cxyz,zmr->xmcyr', row_block.astype(jnp.float32), depth_floats).astype(jnp.bfloat16)
    depth_modes = lax.map(one_block, split_blocks(volume)).reshape(X, M, C, Y, 2)
    row_modes = jnp.einsum('xmcyr,xrkq->mkqcy', depth_modes.astype(jnp.float32), row_table.astype(jnp.float32)).astype(jnp.bfloat16)
    spectrum = jnp.einsum('mkrcy,yrlq->mklqc', row_modes.astype(jnp.float32), column_table.astype(jnp.float32))
    return spectrum.reshape(M * KX, KY, 2, C)

def synthesise(mode_array, row_table, column_table):
    mode_grid = mode_array.reshape(M, KX, KY, 2, C)
    column_part = jnp.einsum('mklqc,yrlq->mkrcy', mode_grid, column_table.astype(jnp.float32), precision=highest).astype(jnp.bfloat16)
    row_part = jnp.einsum('mkqcy,xrkq->xmcyr', column_part.astype(jnp.float32), row_table.astype(jnp.float32)).astype(jnp.bfloat16)
    return row_part.reshape(X // CX, CX, M, C, Y, 2)

def reference(saturation, spectral_weight, pointwise_weight, pointwise_bias, cotangent):
    depth_table = depth_time_table()
    row_table = axis_table(X, KX, 0, X)
    column_table = axis_table(Y, KY, 0, Y)
    depth_floats = depth_table.astype(jnp.float32)
    point_mixer = pointwise_weight.astype(jnp.float32)
    factor = mode_factor(M * KX)[:, None, None, None]
    weight_real = spectral_weight[0]
    weight_imag = spectral_weight[1]
    spectrum = analyse(saturation, depth_table, row_table, column_table)
    mixed_modes = mix(spectrum, weight_real, weight_imag) * factor
    synth_blocks = synthesise(mixed_modes, row_table, column_table)

    def forward_block(pieces):
        row_block, synth_block, cot_block = pieces
        spectral = jnp.einsum('xmcyr,zmr->cxyz', synth_block.astype(jnp.float32), depth_floats)
        preactivation = spectral + jnp.einsum('io,ixyz->oxyz', point_mixer, row_block.astype(jnp.float32)) + pointwise_bias[:, None, None, None]
        output_block = gelu_value(preactivation).astype(jnp.bfloat16)
        slope_block = (cot_block.astype(jnp.float32) * gelu_slope(preactivation)).astype(jnp.bfloat16)
        return (output_block, slope_block)
    output_blocks, slope_blocks = lax.map(forward_block, (split_blocks(saturation), synth_blocks, split_blocks(cotangent)))
    slope_field = join_blocks(slope_blocks)
    upstream = analyse(slope_field, depth_table, row_table, column_table) * factor
    spectral_gradient = outer_gradient(spectrum, upstream)
    returned = back_mix(upstream, weight_real, weight_imag)
    back_blocks = synthesise(returned, row_table, column_table)

    def backward_block(pieces):
        synth_block, slope_block = pieces
        spectral = jnp.einsum('xmcyr,zmr->cxyz', synth_block.astype(jnp.float32), depth_floats)
        return (spectral + jnp.einsum('io,oxyz->ixyz', point_mixer, slope_block.astype(jnp.float32))).astype(jnp.bfloat16)
    gradient_blocks = lax.map(backward_block, (back_blocks, slope_blocks))
    return (join_blocks(output_blocks), join_blocks(gradient_blocks), spectral_gradient)
```

```python
import functools
import math

import jax
import jax.numpy as jnp
import numpy as np
from jax import lax
from jax.experimental import pallas as pl
from jax.experimental.pallas import tpu as pltpu
from jax.sharding import PartitionSpec as P

C = 20
Z = 32
T_SIZE = 8
L = 256
K = 24
KZ = 8
KT = 4
M = 32
G = 16
CY = C * G
VMEM = 48 * 1024 * 1024
BF = jnp.bfloat16
F32 = jnp.float32


def kept_frequency(kept_count):
    position = np.arange(kept_count)
    return np.where(position < kept_count // 2, position, position - kept_count)


def axis_table():
    product = (np.arange(L)[:, None] * kept_frequency(K)[None, :]) % L
    angle = product.astype(np.float32) * np.float32(2.0 * math.pi / L)
    cosine = np.cos(angle) * np.float32(1.0 / math.sqrt(L))
    sine = np.sin(angle) * np.float32(1.0 / math.sqrt(L))
    return np.stack([np.stack([cosine, -sine], -1), np.stack([sine, cosine], -1)], 1)


def depth_table():
    cell = np.arange(Z * T_SIZE)
    depth = ((cell // T_SIZE)[:, None] * kept_frequency(KZ)[None, :] % Z).astype(np.float32) / np.float32(Z)
    time = ((cell % T_SIZE)[:, None] * np.arange(KT)[None, :] % T_SIZE).astype(np.float32) / np.float32(T_SIZE)
    angle = (depth[:, :, None] + time[:, None, :]).reshape(Z * T_SIZE, M) * np.float32(2.0 * math.pi)
    scale = np.float32(1.0 / math.sqrt(Z * T_SIZE))
    table = np.stack([np.cos(angle) * scale, -np.sin(angle) * scale], -1)
    return table.reshape(Z * T_SIZE, 2 * M).T


def row_matrix():
    table = axis_table().reshape(G, 4, 2, 2, 2, 8, 3, 2)
    out = np.zeros((2, 2, 8, 8, G, 4, 2, 2, 2), np.float32)
    part = table.transpose(2, 5, 6, 7, 0, 1, 3, 4).reshape(2, 8, 6, G, 4, 2, 2)
    for pair in range(2):
        out[:, pair, :, :6, :, :, :, pair, :] = part
    return out.reshape(256, 512)


def column_matrix():
    table = axis_table().reshape(G, G, 2, K, 2)
    out = np.zeros((G, G, 8, 2, 128), np.float32)
    for t in range(3):
        for r in range(2):
            out[:, :, 2 * t + r, :, t * K : (t + 1) * K] = table[:, :, r].transpose(1, 0, 3, 2)
    return out.reshape(2048, 256)


def order_matrix():
    out = np.zeros((G, 32, C, G), np.float32)
    for y in range(G):
        for c in range(C):
            out[y, c, c, y] = 1.0
    return out.reshape(512, CY)


def dot(a, b, contract=(1, 0)):
    return lax.dot_general(
        a, b, (((contract[0],), (contract[1],)), ((), ())), preferred_element_type=F32
    )


def pack(first, second):
    first = first.reshape(8, 8, 2 * CY)
    second = second.reshape(8, 8, 2 * CY)
    low = lax.broadcasted_iota(jnp.int32, first.shape, 1) < 4
    even = jnp.where(low, first, pltpu.roll(second, 4, 1))
    odd = jnp.where(low, pltpu.roll(first, 4, 1), second)
    return even, odd


def send_planes(plane, depth, send_ref):
    evens, odds = [], []
    for g in range(2):
        parts = []
        for e in range(2):
            planes = jnp.concatenate([plane(4 * g + e), plane(4 * g + 2 + e)], 0)
            parts.append(dot(depth, planes, (1, 1)))
        even, odd = pack(*parts)
        evens.append(even)
        odds.append(odd)
    send_ref[:, 0] = jnp.concatenate(evens, 1).astype(BF)
    send_ref[:, 1] = jnp.concatenate(odds, 1).astype(BF)


def synthesis(received_ref, g, e, depth):
    rows = received_ref[...].astype(F32)
    even = rows[:, 0, 8 * g : 8 * g + 8]
    odd = rows[:, 1, 8 * g : 8 * g + 8]
    low = lax.broadcasted_iota(jnp.int32, even.shape, 1) < 4
    if e == 0:
        both = jnp.where(low, even, pltpu.roll(odd, 4, 1))
    else:
        both = jnp.where(low, pltpu.roll(even, 4, 1), odd)
    return dot(both.reshape(64, 2 * CY).astype(BF), depth, (0, 0))


def depth_kernel(volume_ref, depth_ref, send_ref):
    send_planes(lambda x: volume_ref[:, x].reshape(CY, L), depth_ref[...], send_ref)


def row_kernel(received_ref, matrix_ref, send_ref):
    product = dot(matrix_ref[...], received_ref[...].reshape(512, 2 * CY))
    total = product[:128] + pltpu.roll(product[128:], CY, 1)
    send_ref[...] = total[:, :CY].reshape(G, 8, CY).astype(BF)


def row_back_kernel(received_ref, matrix_ref, send_ref):
    modes = received_ref[...].astype(F32).reshape(128, CY)
    zeros = jnp.zeros((128, CY), F32)
    upper = jnp.concatenate([modes, zeros], 1)
    lower = jnp.concatenate([zeros, modes], 1)
    both = jnp.concatenate([upper, lower], 0).astype(BF)
    send_ref[...] = dot(matrix_ref[...], both).reshape(G, 32, 2 * CY).astype(BF)


def column_analysis(received_ref, order_ref, column_ref):
    rows = dot(order_ref[...], received_ref[...].reshape(128, CY), (1, 1))
    lanes = jnp.concatenate([rows[32 * y : 32 * y + 32] for y in range(G)], 1)
    return dot(lanes.astype(BF), column_ref[...])


def column_synthesis(modes, order_ref, column_ref, send_ref):
    lanes = dot(modes.astype(BF), column_ref[...], (1, 1))
    rows = jnp.concatenate([lanes[:, 128 * y : 128 * y + 128] for y in range(G)], 0)
    send_ref[...] = dot(rows.astype(BF), order_ref[...], (0, 0)).reshape(G, 8, CY).astype(BF)


def mix_kernel(received_ref, order_ref, column_ref, weight_ref, factor_ref, send_ref, spectrum_ref, mixed_ref):
    spectrum_ref[...] = column_analysis(received_ref, order_ref, column_ref)
    factor = factor_ref[0]
    real = jnp.zeros((C, 128), F32)
    imag = jnp.zeros((C, 128), F32)
    for i in range(C):
        spectrum_real = spectrum_ref[i : i + 1, :128]
        spectrum_imag = spectrum_ref[i : i + 1, 128:]
        weight_real = weight_ref[0, i]
        weight_imag = weight_ref[1, i]
        real += weight_real * spectrum_real - weight_imag * spectrum_imag
        imag += weight_real * spectrum_imag + weight_imag * spectrum_real
    mixed_ref[...] = jnp.zeros((32, 256), F32)
    mixed_ref[:C, :128] = real * factor
    mixed_ref[:C, 128:] = imag * factor
    column_synthesis(mixed_ref[...], order_ref, column_ref, send_ref)


def back_mix_kernel(received_ref, order_ref, column_ref, weight_ref, factor_ref, send_ref, upstream_ref, mixed_ref):
    upstream_ref[...] = column_analysis(received_ref, order_ref, column_ref) * factor_ref[0]
    real = upstream_ref[:C, :128]
    imag = upstream_ref[:C, 128:]
    mixed_ref[...] = jnp.zeros((32, 256), F32)
    for i in range(C):
        weight_real = weight_ref[0, i]
        weight_imag = weight_ref[1, i]
        mixed_ref[i : i + 1, :128] = jnp.sum(weight_real * real + weight_imag * imag, 0, keepdims=True)
        mixed_ref[i : i + 1, 128:] = jnp.sum(weight_real * imag - weight_imag * real, 0, keepdims=True)
    column_synthesis(mixed_ref[...], order_ref, column_ref, send_ref)


def gradient_kernel(spectrum_ref, upstream_ref, gradient_ref):
    real = upstream_ref[:C, :128]
    imag = upstream_ref[:C, 128:]
    for i in range(C):
        spectrum_real = spectrum_ref[i : i + 1, :128]
        spectrum_imag = spectrum_ref[i : i + 1, 128:]
        gradient_ref[0, i] = real * spectrum_real + imag * spectrum_imag
        gradient_ref[1, i] = imag * spectrum_real - real * spectrum_imag


def activation(pre):
    half = jnp.abs(pre) * (1.0 / math.sqrt(2.0))
    bell = jnp.exp(-0.5 * pre * pre)
    t = 1.0 / (1.0 + 0.3275911 * half)
    poly = t * (0.254829592 + t * (-0.284496736 + t * (1.421413741 + t * (-1.453152027 + t * 1.061405429))))
    tail = 0.5 * poly * bell
    return jnp.where(pre < 0.0, tail, 1.0 - tail), bell * (1.0 / math.sqrt(2.0 * math.pi))


def forward_kernel(
    received_ref, volume_ref, cotangent_ref, depth_ref, point_ref, bias_ref, output_ref, slope_ref, send_ref, pre_ref
):
    depth = depth_ref[...]
    point = point_ref[...]
    for g in range(2):
        for e in range(2):
            pre_ref[...] = synthesis(received_ref, g, e, depth)
            for h in range(2):
                x = 4 * g + 2 * h + e
                pre_ref[h * CY : (h + 1) * CY] += dot(point, volume_ref[:, x].reshape(CY, L))

                def step(n, carry):
                    for k in range(2):
                        c = n * 2 + k
                        pre = pre_ref[pl.ds(pl.multiple_of(h * CY + c * G, G), G)] + bias_ref[c]
                        cumulative, density = activation(pre)
                        output_ref[c, x] = (pre * cumulative).astype(BF)
                        slope = cotangent_ref[c, x].astype(F32) * (cumulative + pre * density)
                        slope_ref[c, x] = slope.astype(BF)
                    return carry

                lax.fori_loop(0, C // 2, step, 0)
    send_planes(lambda x: slope_ref[:, x].reshape(CY, L), depth, send_ref)


def backward_kernel(received_ref, slope_ref, depth_ref, point_ref, output_ref):
    depth = depth_ref[...]
    point = point_ref[...]
    for g in range(2):
        for e in range(2):
            spectral = synthesis(received_ref, g, e, depth)
            for h in range(2):
                x = 4 * g + 2 * h + e
                total = spectral[h * CY : (h + 1) * CY] + dot(point, slope_ref[:, x].reshape(CY, L))
                output_ref[:, x] = total.reshape(C, G, L).astype(BF)


def whole(shape):
    return pl.BlockSpec(shape, lambda *_: (0,) * len(shape))


SMEM = pl.BlockSpec(memory_space=pltpu.SMEM)
FIELD = jax.ShapeDtypeStruct((C, G, G, L), BF)
PLANES = pl.BlockSpec((C, 8, G, L), lambda n: (0, n, 0, 0))
BIG = jax.ShapeDtypeStruct((8, 2, 32, 2 * CY), BF)
BIG_ROWS = pl.BlockSpec((8, 2, 16, 2 * CY), lambda n: (0, 0, n, 0))
SMALL = jax.ShapeDtypeStruct((G, 8, CY), BF)
MODES = jax.ShapeDtypeStruct((32, 256), F32)


def call(kernel, out_shape, in_specs=None, out_specs=None, grid=(), scratch=(), flops=0, moved=0):
    extra = {}
    if in_specs is not None:
        extra = {"in_specs": in_specs, "out_specs": out_specs}
    return pl.pallas_call(
        kernel,
        out_shape=out_shape,
        grid=grid,
        scratch_shapes=scratch,
        compiler_params=pltpu.CompilerParams(vmem_limit_bytes=VMEM),
        cost_estimate=pl.CostEstimate(flops=int(flops), bytes_accessed=moved, transcendentals=0),
        **extra,
    )


def exchange_rows(packed):
    moved = lax.all_to_all(packed.reshape(G, 32, 2 * CY), "gx", 0, 0, tiled=True)
    return moved


def exchange_columns(packed):
    return lax.all_to_all(packed, "gy", 0, 0, tiled=True)


def shards(saturation, spectral_weight, pointwise_weight, pointwise_bias, cotangent):
    depth = jnp.asarray(depth_table(), BF)
    rows = jnp.asarray(row_matrix(), BF)
    rows_back = jnp.asarray(row_matrix().T, BF)
    columns = jnp.asarray(column_matrix(), BF)
    order = jnp.asarray(order_matrix(), BF)
    eye = jnp.eye(G, dtype=BF)
    point_back = jnp.kron(pointwise_weight, eye)
    point = jnp.kron(pointwise_weight.T, eye)
    pair = lax.axis_index("gx") * 2 + lax.axis_index("gy") // 8
    factor = jnp.where(pair % KT == 0, 1.0, 2.0).astype(F32).reshape(1)
    weight = jnp.transpose(spectral_weight.reshape(2, 3 * K, C, C), (0, 2, 3, 1))
    weight = jnp.pad(weight, ((0, 0), (0, 0), (0, 0), (0, 128 - 3 * K)))

    depth_call = call(
        depth_kernel, BIG, [PLANES, whole((64, L))], BIG_ROWS, (2,), flops=170e6, moved=3300000
    )
    row_call = call(row_kernel, SMALL, flops=170e6, moved=1000000)
    row_back_call = call(row_back_kernel, jax.ShapeDtypeStruct((G, 32, 2 * CY), BF), flops=170e6, moved=1000000)
    mix_scratch = [pltpu.VMEM((32, 256), F32)]
    vm = pl.BlockSpec(memory_space=pltpu.VMEM)
    mix_specs = [vm, vm, vm, vm, SMEM]
    mix_call = call(mix_kernel, (SMALL, MODES), mix_specs, (vm, vm), (), mix_scratch, 200e6, 2500000)
    back_mix_call = call(back_mix_kernel, (SMALL, MODES), mix_specs, (vm, vm), (), mix_scratch, 200e6, 2500000)
    gradient_call = call(gradient_kernel, jax.ShapeDtypeStruct((2, C, C, 128), F32), flops=1e6, moved=1000000)

    received = exchange_rows(depth_call(saturation, depth))
    received = exchange_columns(row_call(received, rows))
    sent, spectrum = mix_call(received, order, columns, weight, factor)
    received = exchange_columns(sent)
    received = exchange_rows(row_back_call(received, rows_back))
    layer_output, slope, sent = call(
        forward_kernel,
        (FIELD, FIELD, BIG),
        [BIG_ROWS, PLANES, PLANES, whole((64, L)), whole((CY, CY)), SMEM],
        (PLANES, PLANES, BIG_ROWS),
        (2,),
        [pltpu.VMEM((2 * CY, L), F32)],
        1500e6,
        12000000,
    )(received.reshape(BIG.shape), saturation, cotangent, depth, point, pointwise_bias)
    received = exchange_rows(sent)
    received = exchange_columns(row_call(received, rows))
    sent, upstream = back_mix_call(received, order, columns, weight, factor)
    gradient = gradient_call(spectrum, upstream)
    received = exchange_columns(sent)
    received = exchange_rows(row_back_call(received, rows_back))
    input_gradient = call(
        backward_kernel,
        FIELD,
        [BIG_ROWS, PLANES, whole((64, L)), whole((CY, CY))],
        PLANES,
        (2,),
        (),
        1300e6,
        6000000,
    )(received.reshape(BIG.shape), slope, depth, point_back)
    gradient = jnp.transpose(gradient[..., : 3 * K], (0, 3, 1, 2)).reshape(2, 3, K, C, C)
    return layer_output, input_gradient, gradient


def solution(mesh):
    return jax.shard_map(
        shards,
        mesh=mesh,
        in_specs=(
            P(None, "gx", "gy", None),
            P(None, ("gx", "gy"), None, None, None),
            P(),
            P(),
            P(None, "gx", "gy", None),
        ),
        out_specs=(
            P(None, "gx", "gy", None),
            P(None, "gx", "gy", None),
            P(None, ("gx", "gy"), None, None, None),
        ),
        check_vma=False,
    )
```

```python
import functools
import math

import jax
import jax.numpy as jnp
import numpy as np
from jax import lax
from jax.experimental import pallas as pl
from jax.experimental.pallas import tpu as pltpu
from jax.sharding import PartitionSpec as P

C = 20
Z = 32
T_SIZE = 8
L = 256
K = 24
KZ = 8
KT = 4
M = 32
G = 16
CY = C * G
MIB = 1024 * 1024
BF = jnp.bfloat16
F32 = jnp.float32


def kept_frequency(kept_count):
    position = np.arange(kept_count)
    return np.where(position < kept_count // 2, position, position - kept_count)


def axis_table():
    product = (np.arange(L)[:, None] * kept_frequency(K)[None, :]) % L
    angle = product.astype(np.float32) * np.float32(2.0 * math.pi / L)
    cosine = np.cos(angle) * np.float32(1.0 / math.sqrt(L))
    sine = np.sin(angle) * np.float32(1.0 / math.sqrt(L))
    return np.stack([np.stack([cosine, -sine], -1), np.stack([sine, cosine], -1)], 1)


def depth_table():
    cell = np.arange(Z * T_SIZE)
    depth = ((cell // T_SIZE)[:, None] * kept_frequency(KZ)[None, :] % Z).astype(np.float32) / np.float32(Z)
    time = ((cell % T_SIZE)[:, None] * np.arange(KT)[None, :] % T_SIZE).astype(np.float32) / np.float32(T_SIZE)
    angle = (depth[:, :, None] + time[:, None, :]).reshape(Z * T_SIZE, M) * np.float32(2.0 * math.pi)
    scale = np.float32(1.0 / math.sqrt(Z * T_SIZE))
    table = np.stack([np.cos(angle) * scale, -np.sin(angle) * scale], -1)
    return table.reshape(Z * T_SIZE, 2 * M).T


def row_matrix():
    table = axis_table().reshape(G, 4, 2, 2, 2, 8, 3, 2)
    out = np.zeros((2, 2, 8, 8, G, 4, 2, 2, 2), np.float32)
    part = table.transpose(2, 5, 6, 7, 0, 1, 3, 4).reshape(2, 8, 6, G, 4, 2, 2)
    for pair in range(2):
        out[:, pair, :, :6, :, :, :, pair, :] = part
    return out.reshape(256, 512)


def column_matrix():
    table = axis_table().reshape(G, G, 2, K, 2)
    out = np.zeros((G, G, 8, 2, 128), np.float32)
    for t in range(3):
        for r in range(2):
            out[:, :, 2 * t + r, :, t * K : (t + 1) * K] = table[:, :, r].transpose(1, 0, 3, 2)
    return out.reshape(2048, 256)


def order_matrix():
    out = np.zeros((G, 32, C, G), np.float32)
    for y in range(G):
        for c in range(C):
            out[y, c, c, y] = 1.0
    return out.reshape(512, CY)


def dot(a, b, contract=(1, 0)):
    return lax.dot_general(
        a, b, (((contract[0],), (contract[1],)), ((), ())), preferred_element_type=F32
    )


def pack(first, second):
    first = first.reshape(8, 8, 2 * CY)
    second = second.reshape(8, 8, 2 * CY)
    low = lax.broadcasted_iota(jnp.int32, first.shape, 1) < 4
    even = jnp.where(low, first, pltpu.roll(second, 4, 1))
    odd = jnp.where(low, pltpu.roll(first, 4, 1), second)
    return even, odd


def send_planes(plane, depth, send_ref):
    evens, odds = [], []
    for g in range(2):
        parts = []
        for e in range(2):
            planes = jnp.concatenate([plane(4 * g + e), plane(4 * g + 2 + e)], 0)
            parts.append(dot(depth, planes, (1, 1)))
        even, odd = pack(*parts)
        evens.append(even)
        odds.append(odd)
    send_ref[:, 0] = jnp.concatenate(evens, 1).astype(BF)
    send_ref[:, 1] = jnp.concatenate(odds, 1).astype(BF)


def synthesis(rows, g, e, depth):
    even = rows[:, 0, 8 * g : 8 * g + 8]
    odd = rows[:, 1, 8 * g : 8 * g + 8]
    low = lax.broadcasted_iota(jnp.int32, even.shape, 1) < 4
    if e == 0:
        both = jnp.where(low, even, pltpu.roll(odd, 4, 1))
    else:
        both = jnp.where(low, pltpu.roll(even, 4, 1), odd)
    return dot(both.reshape(64, 2 * CY).astype(BF), depth, (0, 0))


def depth_kernel(volume_ref, depth_ref, send_ref):
    send_planes(lambda x: volume_ref[:, x].reshape(CY, L), depth_ref[...], send_ref)


def row_kernel(received_ref, matrix_ref, send_ref):
    product = dot(matrix_ref[...], received_ref[...].reshape(512, 2 * CY))
    total = product[:128] + pltpu.roll(product[128:], CY, 1)
    send_ref[...] = total[:, :CY].reshape(G, 8, CY).astype(BF)


def row_back_kernel(received_ref, matrix_ref, send_ref):
    modes = received_ref[...].astype(F32).reshape(128, CY)
    zeros = jnp.zeros((128, CY), F32)
    upper = jnp.concatenate([modes, zeros], 1)
    lower = jnp.concatenate([zeros, modes], 1)
    both = jnp.concatenate([upper, lower], 0).astype(BF)
    send_ref[...] = dot(matrix_ref[...], both).reshape(G, 32, 2 * CY).astype(BF)


def column_analysis(received_ref, order_ref, column_ref):
    rows = dot(order_ref[...], received_ref[...].reshape(128, CY), (1, 1))
    lanes = jnp.concatenate([rows[32 * y : 32 * y + 32] for y in range(G)], 1)
    return dot(lanes.astype(BF), column_ref[...])


def column_synthesis(modes, order_ref, column_ref, send_ref):
    lanes = dot(modes.astype(BF), column_ref[...], (1, 1))
    rows = jnp.concatenate([lanes[:, 128 * y : 128 * y + 128] for y in range(G)], 0)
    send_ref[...] = dot(rows.astype(BF), order_ref[...], (0, 0)).reshape(G, 8, CY).astype(BF)


def mix_kernel(received_ref, order_ref, column_ref, weight_ref, factor_ref, send_ref, spectrum_ref, mixed_ref):
    spectrum_ref[...] = column_analysis(received_ref, order_ref, column_ref)
    factor = factor_ref[0]
    real = jnp.zeros((C, 128), F32)
    imag = jnp.zeros((C, 128), F32)
    for i in range(C):
        spectrum_real = spectrum_ref[i : i + 1, :128]
        spectrum_imag = spectrum_ref[i : i + 1, 128:]
        weight_real = weight_ref[0, i]
        weight_imag = weight_ref[1, i]
        real += weight_real * spectrum_real - weight_imag * spectrum_imag
        imag += weight_real * spectrum_imag + weight_imag * spectrum_real
    mixed_ref[...] = jnp.zeros((32, 256), F32)
    mixed_ref[:C, :128] = real * factor
    mixed_ref[:C, 128:] = imag * factor
    column_synthesis(mixed_ref[...], order_ref, column_ref, send_ref)


def back_mix_kernel(received_ref, order_ref, column_ref, weight_ref, factor_ref, send_ref, upstream_ref, mixed_ref):
    upstream_ref[...] = column_analysis(received_ref, order_ref, column_ref) * factor_ref[0]
    real = upstream_ref[:C, :128]
    imag = upstream_ref[:C, 128:]
    mixed_ref[...] = jnp.zeros((32, 256), F32)
    for i in range(C):
        weight_real = weight_ref[0, i]
        weight_imag = weight_ref[1, i]
        mixed_ref[i : i + 1, :128] = jnp.sum(weight_real * real + weight_imag * imag, 0, keepdims=True)
        mixed_ref[i : i + 1, 128:] = jnp.sum(weight_real * imag - weight_imag * real, 0, keepdims=True)
    column_synthesis(mixed_ref[...], order_ref, column_ref, send_ref)


def gradient_kernel(spectrum_ref, upstream_ref, gradient_ref):
    real = upstream_ref[:C, :128]
    imag = upstream_ref[:C, 128:]
    for i in range(C):
        spectrum_real = spectrum_ref[i : i + 1, :128]
        spectrum_imag = spectrum_ref[i : i + 1, 128:]
        gradient_ref[0, i] = real * spectrum_real + imag * spectrum_imag
        gradient_ref[1, i] = imag * spectrum_real - real * spectrum_imag


def activation(pre):
    cumulative = 0.5 + 0.5 * lax.erf(pre * (1.0 / math.sqrt(2.0)))
    density = jnp.exp(-0.5 * pre * pre) * (1.0 / math.sqrt(2.0 * math.pi))
    return cumulative, density


def forward_kernel(
    received_ref, volume_ref, cotangent_ref, depth_ref, point_ref, bias_ref, output_ref, slope_ref, send_ref
):
    depth = depth_ref[...]
    point = point_ref[...]
    rows = received_ref[...].astype(F32)
    for g in range(2):
        for e in range(2):
            spectral = synthesis(rows, g, e, depth)
            for h in range(2):
                x = 4 * g + 2 * h + e
                total = spectral[h * CY : (h + 1) * CY] + dot(point, volume_ref[:, x].reshape(CY, L))
                for c in range(C):
                    pre = total[c * G : (c + 1) * G] + bias_ref[c]
                    cumulative, density = activation(pre)
                    output_ref[c, x] = (pre * cumulative).astype(BF)
                    slope = cotangent_ref[c, x].astype(F32) * (cumulative + pre * density)
                    slope_ref[c, x] = slope.astype(BF)
    send_planes(lambda x: slope_ref[:, x].reshape(CY, L), depth, send_ref)


def backward_kernel(received_ref, slope_ref, depth_ref, point_ref, output_ref):
    depth = depth_ref[...]
    point = point_ref[...]
    rows = received_ref[...].astype(F32)
    for g in range(2):
        for e in range(2):
            spectral = synthesis(rows, g, e, depth)
            for h in range(2):
                x = 4 * g + 2 * h + e
                total = spectral[h * CY : (h + 1) * CY] + dot(point, slope_ref[:, x].reshape(CY, L))
                output_ref[:, x] = total.reshape(C, G, L).astype(BF)


def whole(shape):
    return pl.BlockSpec(shape, lambda *_: (0,) * len(shape))


SMEM = pl.BlockSpec(memory_space=pltpu.SMEM)
FIELD = jax.ShapeDtypeStruct((C, G, G, L), BF)
PLANES = pl.BlockSpec((C, 8, G, L), lambda n: (0, n, 0, 0))
BIG = jax.ShapeDtypeStruct((8, 2, 32, 2 * CY), BF)
BIG_ROWS = pl.BlockSpec((8, 2, 16, 2 * CY), lambda n: (0, 0, n, 0))
SMALL = jax.ShapeDtypeStruct((G, 8, CY), BF)
MODES = jax.ShapeDtypeStruct((32, 256), F32)


def call(kernel, out_shape, in_specs=None, out_specs=None, grid=(), scratch=(), flops=0, moved=0, room=16):
    extra = {}
    if in_specs is not None:
        extra = {"in_specs": in_specs, "out_specs": out_specs}
    return pl.pallas_call(
        kernel,
        out_shape=out_shape,
        grid=grid,
        scratch_shapes=scratch,
        compiler_params=pltpu.CompilerParams(vmem_limit_bytes=room * MIB),
        cost_estimate=pl.CostEstimate(flops=int(flops), bytes_accessed=moved, transcendentals=0),
        **extra,
    )


def exchange_rows(packed):
    moved = lax.all_to_all(packed.reshape(G, 32, 2 * CY), "gx", 0, 0, tiled=True)
    return moved


def exchange_columns(packed):
    return lax.all_to_all(packed, "gy", 0, 0, tiled=True)


def shards(saturation, spectral_weight, pointwise_weight, pointwise_bias, cotangent):
    depth = jnp.asarray(depth_table(), BF)
    rows = jnp.asarray(row_matrix(), BF)
    rows_back = jnp.asarray(row_matrix().T, BF)
    columns = jnp.asarray(column_matrix(), BF)
    order = jnp.asarray(order_matrix(), BF)
    eye = jnp.eye(G, dtype=BF)
    point_back = jnp.kron(pointwise_weight, eye)
    point = jnp.kron(pointwise_weight.T, eye)
    pair = lax.axis_index("gx") * 2 + lax.axis_index("gy") // 8
    factor = jnp.where(pair % KT == 0, 1.0, 2.0).astype(F32).reshape(1)
    weight = jnp.transpose(spectral_weight.reshape(2, 3 * K, C, C), (0, 2, 3, 1))
    weight = jnp.pad(weight, ((0, 0), (0, 0), (0, 0), (0, 128 - 3 * K)))

    depth_call = call(
        depth_kernel, BIG, [PLANES, whole((64, L))], BIG_ROWS, (2,), flops=170e6, moved=3300000, room=60
    )
    row_call = call(row_kernel, SMALL, flops=170e6, moved=1000000)
    row_back_call = call(row_back_kernel, jax.ShapeDtypeStruct((G, 32, 2 * CY), BF), flops=170e6, moved=1000000)
    mix_scratch = [pltpu.VMEM((32, 256), F32)]
    vm = pl.BlockSpec(memory_space=pltpu.VMEM)
    mix_specs = [vm, vm, vm, vm, SMEM]
    mix_call = call(mix_kernel, (SMALL, MODES), mix_specs, (vm, vm), (), mix_scratch, 200e6, 2500000)
    back_mix_call = call(back_mix_kernel, (SMALL, MODES), mix_specs, (vm, vm), (), mix_scratch, 200e6, 2500000)
    gradient_call = call(gradient_kernel, jax.ShapeDtypeStruct((2, C, C, 128), F32), flops=1e6, moved=1000000)

    received = exchange_rows(depth_call(saturation, depth))
    received, weight = lax.optimization_barrier((received, weight))
    received = exchange_columns(row_call(received, rows))
    sent, spectrum = mix_call(received, order, columns, weight, factor)
    received = exchange_columns(sent)
    received = exchange_rows(row_back_call(received, rows_back))
    layer_output, slope, sent = call(
        forward_kernel,
        (FIELD, FIELD, BIG),
        [BIG_ROWS, PLANES, PLANES, whole((64, L)), whole((CY, CY)), SMEM],
        (PLANES, PLANES, BIG_ROWS),
        (2,),
        (),
        1500e6,
        12000000,
        60,
    )(received.reshape(BIG.shape), saturation, cotangent, depth, point, pointwise_bias)
    received = exchange_rows(sent)
    received = exchange_columns(row_call(received, rows))
    sent, upstream = back_mix_call(received, order, columns, weight, factor)
    gradient = gradient_call(spectrum, upstream)
    received = exchange_columns(sent)
    received = exchange_rows(row_back_call(received, rows_back))
    input_gradient = call(
        backward_kernel,
        FIELD,
        [BIG_ROWS, PLANES, whole((64, L)), whole((CY, CY))],
        PLANES,
        (2,),
        (),
        1300e6,
        6000000,
        20,
    )(received.reshape(BIG.shape), slope, depth, point_back)
    gradient = jnp.transpose(gradient[..., : 3 * K], (0, 3, 1, 2)).reshape(2, 3, K, C, C)
    return layer_output, input_gradient, gradient


def solution(mesh):
    return jax.shard_map(
        shards,
        mesh=mesh,
        in_specs=(
            P(None, "gx", "gy", None),
            P(None, ("gx", "gy"), None, None, None),
            P(),
            P(),
            P(None, "gx", "gy", None),
        ),
        out_specs=(
            P(None, "gx", "gy", None),
            P(None, "gx", "gy", None),
            P(None, ("gx", "gy"), None, None, None),
        ),
        check_vma=False,
    )
```

```python
import functools
import math

import jax
import jax.numpy as jnp
import numpy as np
from jax import lax
from jax.experimental import pallas as pl
from jax.experimental.pallas import tpu as pltpu
from jax.sharding import PartitionSpec as P

C = 20
Z = 32
T_SIZE = 8
L = 256
K = 24
KZ = 8
KT = 4
M = 32
G = 16
CY = C * G
MIB = 1024 * 1024
BF = jnp.bfloat16
F32 = jnp.float32


def kept_frequency(kept_count):
    position = np.arange(kept_count)
    return np.where(position < kept_count // 2, position, position - kept_count)


def axis_table():
    product = (np.arange(L)[:, None] * kept_frequency(K)[None, :]) % L
    angle = product.astype(np.float32) * np.float32(2.0 * math.pi / L)
    cosine = np.cos(angle) * np.float32(1.0 / math.sqrt(L))
    sine = np.sin(angle) * np.float32(1.0 / math.sqrt(L))
    return np.stack([np.stack([cosine, -sine], -1), np.stack([sine, cosine], -1)], 1)


def depth_table():
    cell = np.arange(Z * T_SIZE)
    depth = ((cell // T_SIZE)[:, None] * kept_frequency(KZ)[None, :] % Z).astype(np.float32) / np.float32(Z)
    time = ((cell % T_SIZE)[:, None] * np.arange(KT)[None, :] % T_SIZE).astype(np.float32) / np.float32(T_SIZE)
    angle = (depth[:, :, None] + time[:, None, :]).reshape(Z * T_SIZE, M) * np.float32(2.0 * math.pi)
    scale = np.float32(1.0 / math.sqrt(Z * T_SIZE))
    table = np.stack([np.cos(angle) * scale, -np.sin(angle) * scale], -1)
    return table.reshape(Z * T_SIZE, 2 * M).T


def row_matrix():
    table = axis_table().reshape(G, 4, 2, 2, 2, 8, 3, 2)
    out = np.zeros((2, 2, 8, 8, G, 4, 2, 2, 2), np.float32)
    part = table.transpose(2, 5, 6, 7, 0, 1, 3, 4).reshape(2, 8, 6, G, 4, 2, 2)
    for pair in range(2):
        out[:, pair, :, :6, :, :, :, pair, :] = part
    return out.reshape(256, 512)


def column_matrix():
    table = axis_table().reshape(G, G, 2, K, 2)
    out = np.zeros((G, G, 8, 2, 128), np.float32)
    for t in range(3):
        for r in range(2):
            out[:, :, 2 * t + r, :, t * K : (t + 1) * K] = table[:, :, r].transpose(1, 0, 3, 2)
    return out.reshape(2048, 256)


def order_matrix():
    out = np.zeros((G, 32, C, G), np.float32)
    for y in range(G):
        for c in range(C):
            out[y, c, c, y] = 1.0
    return out.reshape(512, CY)


def dot(a, b, contract=(1, 0)):
    return lax.dot_general(
        a, b, (((contract[0],), (contract[1],)), ((), ())), preferred_element_type=F32
    )


def pack(first, second):
    first = first.reshape(8, 8, 2 * CY)
    second = second.reshape(8, 8, 2 * CY)
    low = lax.broadcasted_iota(jnp.int32, first.shape, 1) < 4
    even = jnp.where(low, first, pltpu.roll(second, 4, 1))
    odd = jnp.where(low, pltpu.roll(first, 4, 1), second)
    return even, odd


def packed_planes(plane, depth):
    return pack(*[dot(depth, jnp.concatenate([plane(e), plane(2 + e)], 0), (1, 1)) for e in range(2)])


def send_planes(tiles, send_ref, rows):
    for parity in range(2):
        send_ref[:, parity, rows] = jnp.concatenate([tiles[0][parity], tiles[1][parity]], 1).astype(BF)


def synthesis(rows, g, e, depth):
    even = rows[:, 0, 8 * g : 8 * g + 8]
    odd = rows[:, 1, 8 * g : 8 * g + 8]
    low = lax.broadcasted_iota(jnp.int32, even.shape, 1) < 4
    if e == 0:
        both = jnp.where(low, even, pltpu.roll(odd, 4, 1))
    else:
        both = jnp.where(low, pltpu.roll(even, 4, 1), odd)
    return dot(both.reshape(64, 2 * CY).astype(BF), depth, (0, 0))


def depth_kernel(volume_ref, depth_ref, send_ref):
    depth = depth_ref[...]
    tiles = [packed_planes(lambda k: volume_ref[:, 4 * g + k].reshape(CY, L), depth) for g in range(2)]
    send_planes(tiles, send_ref, slice(0, 16))


def row_kernel(received_ref, matrix_ref, send_ref):
    product = dot(matrix_ref[...], received_ref[...].reshape(512, 2 * CY))
    total = product[:128] + pltpu.roll(product[128:], CY, 1)
    send_ref[...] = total[:, :CY].reshape(G, 8, CY).astype(BF)


def row_back_kernel(received_ref, matrix_ref, send_ref):
    modes = received_ref[...].astype(F32).reshape(128, CY)
    zeros = jnp.zeros((128, CY), F32)
    upper = jnp.concatenate([modes, zeros], 1)
    lower = jnp.concatenate([zeros, modes], 1)
    both = jnp.concatenate([upper, lower], 0).astype(BF)
    send_ref[...] = dot(matrix_ref[...], both).reshape(G, 32, 2 * CY).astype(BF)


def column_analysis(received_ref, order_ref, column_ref):
    rows = dot(order_ref[...], received_ref[...].reshape(128, CY), (1, 1))
    lanes = jnp.concatenate([rows[32 * y : 32 * y + 32] for y in range(G)], 1)
    return dot(lanes.astype(BF), column_ref[...])


def column_synthesis(modes, order_ref, column_ref, send_ref):
    lanes = dot(modes.astype(BF), column_ref[...], (1, 1))
    rows = jnp.concatenate([lanes[:, 128 * y : 128 * y + 128] for y in range(G)], 0)
    send_ref[...] = dot(rows.astype(BF), order_ref[...], (0, 0)).reshape(G, 8, CY).astype(BF)


def weight_rows(weight_ref, i):
    spare = jnp.zeros((2 * C, 128 - 3 * K), F32)
    return jnp.concatenate([weight_ref[0, i], weight_ref[1, i], weight_ref[2, i], spare], 1)


def partner(rows):
    part = lax.broadcasted_iota(jnp.int32, rows.shape, 0) % 2
    return part == 0, jnp.where(part == 0, pltpu.roll(rows, 2 * C - 1, 0), pltpu.roll(rows, 1, 0))


def mode_factor():
    pair = lax.axis_index("gx") * 2 + lax.axis_index("gy") // 8
    return jnp.where(pair % KT == 0, 1.0, 2.0).astype(F32)


def mix_kernel(
    received_ref, order_ref, column_ref, weight_ref, send_ref, spectrum_ref, mixed_ref, parts_ref
):
    spectrum_ref[...] = column_analysis(received_ref, order_ref, column_ref)
    by_real = jnp.zeros((2 * C, 128), F32)
    by_imag = jnp.zeros((2 * C, 128), F32)
    for i in range(C):
        weight = weight_rows(weight_ref, i)
        by_real += weight * spectrum_ref[i : i + 1, :128]
        by_imag += weight * spectrum_ref[i : i + 1, 128:]
    is_real, other = partner(by_imag)
    parts_ref[...] = (by_real + jnp.where(is_real, -other, other)) * mode_factor()
    mixed_ref[...] = jnp.zeros((32, 256), F32)
    mixed_ref[:C, :128] = parts_ref[pl.ds(0, C, stride=2), :]
    mixed_ref[:C, 128:] = parts_ref[pl.ds(1, C, stride=2), :]
    column_synthesis(mixed_ref[...], order_ref, column_ref, send_ref)


def back_mix_kernel(
    received_ref, order_ref, column_ref, weight_ref, spectrum_ref,
    send_ref, gradient_ref, mixed_ref, parts_ref,
):
    mixed_ref[...] = column_analysis(received_ref, order_ref, column_ref) * mode_factor()
    parts_ref[pl.ds(0, C, stride=2), :] = mixed_ref[:C, :128]
    parts_ref[pl.ds(1, C, stride=2), :] = mixed_ref[:C, 128:]
    upstream = parts_ref[...]
    is_real, other = partner(upstream)
    turned = jnp.where(is_real, other, -other)
    mixed_ref[...] = jnp.zeros((32, 256), F32)
    for i in range(C):
        weight = weight_rows(weight_ref, i)
        mixed_ref[i : i + 1, :128] = jnp.sum(weight * upstream, 0, keepdims=True)
        mixed_ref[i : i + 1, 128:] = jnp.sum(weight * turned, 0, keepdims=True)
    column_synthesis(mixed_ref[...], order_ref, column_ref, send_ref)
    for i in range(C):
        gradient = upstream * spectrum_ref[i : i + 1, :128] + turned * spectrum_ref[i : i + 1, 128:]
        for t in range(3):
            gradient_ref[t, i] = gradient[:, t * K : (t + 1) * K]


def activation(pre):
    cumulative = 0.5 + 0.5 * lax.erf(pre * (1.0 / math.sqrt(2.0)))
    density = jnp.exp(-0.5 * pre * pre) * (1.0 / math.sqrt(2.0 * math.pi))
    return cumulative, density


def spread_point(point_ref, side):
    row = lax.broadcasted_iota(jnp.int32, (CY, C), 0) // G
    repeat = jnp.where(row == lax.broadcasted_iota(jnp.int32, (CY, C), 1), 1.0, 0.0).astype(BF)
    tall = dot(repeat, point_ref[...], (1, 1 - side)).astype(BF)
    wide = dot(tall, repeat, (1, 1))
    row = lax.broadcasted_iota(jnp.int32, (CY, CY), 0) % G
    column = lax.broadcasted_iota(jnp.int32, (CY, CY), 1) % G
    return jnp.where(row == column, wide, 0.0).astype(BF)


def leave(made_ref, output_ref, left, block):
    planes = pl.ds(4 * block, 4)
    return pltpu.make_async_copy(made_ref.at[:, planes], output_ref.at[:, planes], left.at[block])


def half_rows(received_ref, half):
    return received_ref[:, :, pl.ds(pl.multiple_of(16 * half, 16), 16), :].astype(F32)


def forward_kernel(
    received_ref, volume_ref, cotangent_ref, depth_ref, point_ref, bias_ref,
    output_ref, slope_ref, send_ref, wide_ref, made_ref, left,
):
    depth = depth_ref[...]
    wide_ref[...] = spread_point(point_ref, 0)

    def step(half, carry):
        rows = half_rows(received_ref, half)
        point = wide_ref[...]
        tiles = []
        for g in range(2):
            first = 8 * half + 4 * g
            for e in range(2):
                spectral = synthesis(rows, g, e, depth)
                for h in range(2):
                    x = first + 2 * h + e
                    total = spectral[h * CY : (h + 1) * CY] + dot(point, volume_ref[:, x].reshape(CY, L))
                    for c in range(C):
                        pre = total[c * G : (c + 1) * G] + bias_ref[c]
                        cumulative, density = activation(pre)
                        made_ref[c, x] = (pre * cumulative).astype(BF)
                        slope = cotangent_ref[c, x].astype(F32) * (cumulative + pre * density)
                        slope_ref[c, x] = slope.astype(BF)
            leave(made_ref, output_ref, left, 2 * half + g).start()
            tiles.append(packed_planes(lambda k: slope_ref[:, first + k].reshape(CY, L), depth))
        send_planes(tiles, send_ref, pl.ds(pl.multiple_of(16 * half, 16), 16))
        return carry

    lax.fori_loop(0, 2, step, 0)
    for block in range(4):
        leave(made_ref, output_ref, left, block).wait()


def backward_kernel(received_ref, slope_ref, depth_ref, point_ref, output_ref, made_ref, left):
    depth = depth_ref[...]
    point = spread_point(point_ref, 1)
    for half in range(2):
        rows = half_rows(received_ref, half)
        for g in range(2):
            first = 8 * half + 4 * g
            for e in range(2):
                spectral = synthesis(rows, g, e, depth)
                for h in range(2):
                    x = first + 2 * h + e
                    total = spectral[h * CY : (h + 1) * CY] + dot(point, slope_ref[:, x].reshape(CY, L))
                    made_ref[:, x] = total.reshape(C, G, L).astype(BF)
            leave(made_ref, output_ref, left, 2 * half + g).start()
    for block in range(4):
        leave(made_ref, output_ref, left, block).wait()


SMEM = pl.BlockSpec(memory_space=pltpu.SMEM)
NEAR = pl.BlockSpec(memory_space=pltpu.VMEM)
FAR = pl.BlockSpec(memory_space=pl.ANY)
FIELD = jax.ShapeDtypeStruct((C, G, G, L), BF)
HELD = pltpu.VMEM((C, G, G, L), BF)
FOUR = pltpu.SemaphoreType.DMA((4,))
BIG = jax.ShapeDtypeStruct((8, 2, 32, 2 * CY), BF)
SMALL = jax.ShapeDtypeStruct((G, 8, CY), BF)
MODES = jax.ShapeDtypeStruct((32, 256), F32)


def call(kernel, out_shape, in_specs=None, out_specs=None, scratch=(), flops=0, moved=0, room=16, grid=()):
    extra = {}
    if in_specs is not None:
        extra = {"in_specs": in_specs, "out_specs": out_specs}
    return pl.pallas_call(
        kernel,
        out_shape=out_shape,
        grid=grid,
        scratch_shapes=scratch,
        compiler_params=pltpu.CompilerParams(vmem_limit_bytes=room * MIB),
        cost_estimate=pl.CostEstimate(flops=int(flops), bytes_accessed=moved, transcendentals=0),
        **extra,
    )


def exchange_rows(packed):
    moved = lax.all_to_all(packed.reshape(G, 32, 2 * CY), "gx", 0, 0, tiled=True)
    return moved


def exchange_columns(packed):
    return lax.all_to_all(packed, "gy", 0, 0, tiled=True)


def shards(saturation, spectral_weight, pointwise_weight, pointwise_bias, cotangent):
    depth = jnp.asarray(depth_table(), BF)
    rows = jnp.asarray(row_matrix(), BF)
    rows_back = jnp.asarray(row_matrix().T, BF)
    columns = jnp.asarray(column_matrix(), BF)
    order = jnp.asarray(order_matrix(), BF)
    weight = jnp.transpose(spectral_weight, (1, 3, 4, 0, 2)).reshape(3, C, 2 * C, K)

    depth_call = call(
        depth_kernel,
        BIG,
        [pl.BlockSpec((C, 8, G, L), lambda n: (0, n, 0, 0)), pl.BlockSpec((64, L), lambda n: (0, 0))],
        pl.BlockSpec((8, 2, 16, 2 * CY), lambda n: (0, 0, n, 0)),
        flops=170e6,
        moved=3300000,
        room=60,
        grid=(2,),
    )
    row_call = call(row_kernel, SMALL, flops=170e6, moved=1000000)
    row_back_call = call(row_back_kernel, jax.ShapeDtypeStruct((G, 32, 2 * CY), BF), flops=170e6, moved=1000000)
    mix_scratch = [pltpu.VMEM((32, 256), F32), pltpu.VMEM((2 * C, 128), F32)]
    mix_call = call(mix_kernel, (SMALL, MODES), [NEAR] * 4, (NEAR, NEAR), mix_scratch, 200e6, 2500000)
    back_mix_call = call(
        back_mix_kernel,
        (SMALL, jax.ShapeDtypeStruct((3, C, 2 * C, K), F32)),
        [NEAR] * 5,
        (NEAR, NEAR),
        mix_scratch,
        200e6,
        4000000,
    )

    received = exchange_rows(depth_call(saturation, depth))
    received = exchange_columns(row_call(received, rows))
    sent, spectrum = mix_call(received, order, columns, weight)
    received = exchange_columns(sent)
    received = exchange_rows(row_back_call(received, rows_back))
    layer_output, slope, sent = call(
        forward_kernel,
        (FIELD, FIELD, BIG),
        [NEAR] * 5 + [SMEM],
        (FAR, NEAR, NEAR),
        [pltpu.VMEM((CY, CY), BF), HELD, FOUR],
        1500e6,
        12000000,
        20,
    )(received.reshape(BIG.shape), saturation, cotangent, depth, pointwise_weight, pointwise_bias)
    received = exchange_rows(sent)
    received = exchange_columns(row_call(received, rows))
    sent, gradient = back_mix_call(received, order, columns, weight, spectrum)
    received = exchange_columns(sent)
    received = exchange_rows(row_back_call(received, rows_back))
    input_gradient = call(
        backward_kernel,
        FIELD,
        [NEAR] * 4,
        FAR,
        [HELD, FOUR],
        1300e6,
        6000000,
        16,
    )(received.reshape(BIG.shape), slope, depth, pointwise_weight)
    gradient = jnp.transpose(gradient.reshape(3, C, C, 2, K), (3, 0, 4, 1, 2))
    return layer_output, input_gradient, gradient


def solution(mesh):
    return jax.shard_map(
        shards,
        mesh=mesh,
        in_specs=(
            P(None, "gx", "gy", None),
            P(None, ("gx", "gy"), None, None, None),
            P(),
            P(),
            P(None, "gx", "gy", None),
        ),
        out_specs=(
            P(None, "gx", "gy", None),
            P(None, "gx", "gy", None),
            P(None, ("gx", "gy"), None, None, None),
        ),
        check_vma=False,
    )
```

```python
import functools
import math

import jax
import jax.numpy as jnp
import numpy as np
from jax import lax
from jax.experimental import pallas as pl
from jax.experimental.pallas import tpu as pltpu
from jax.sharding import PartitionSpec as P

C = 20
Z = 32
T_SIZE = 8
L = 256
K = 24
KZ = 8
KT = 4
M = 32
G = 16
CY = C * G
MIB = 1024 * 1024
BF = jnp.bfloat16
F32 = jnp.float32


def kept_frequency(kept_count):
    position = np.arange(kept_count)
    return np.where(position < kept_count // 2, position, position - kept_count)


def axis_table():
    product = (np.arange(L)[:, None] * kept_frequency(K)[None, :]) % L
    angle = product.astype(np.float32) * np.float32(2.0 * math.pi / L)
    cosine = np.cos(angle) * np.float32(1.0 / math.sqrt(L))
    sine = np.sin(angle) * np.float32(1.0 / math.sqrt(L))
    return np.stack([np.stack([cosine, -sine], -1), np.stack([sine, cosine], -1)], 1)


def depth_table():
    cell = np.arange(Z * T_SIZE)
    depth = ((cell // T_SIZE)[:, None] * kept_frequency(KZ)[None, :] % Z).astype(np.float32) / np.float32(Z)
    time = ((cell % T_SIZE)[:, None] * np.arange(KT)[None, :] % T_SIZE).astype(np.float32) / np.float32(T_SIZE)
    angle = (depth[:, :, None] + time[:, None, :]).reshape(Z * T_SIZE, M) * np.float32(2.0 * math.pi)
    scale = np.float32(1.0 / math.sqrt(Z * T_SIZE))
    table = np.stack([np.cos(angle) * scale, -np.sin(angle) * scale], -1)
    return table.reshape(Z * T_SIZE, 2 * M).T


def row_matrix():
    table = axis_table().reshape(G, 4, 2, 2, 2, 8, 3, 2)
    out = np.zeros((2, 2, 8, 8, G, 4, 2, 2, 2), np.float32)
    part = table.transpose(2, 5, 6, 7, 0, 1, 3, 4).reshape(2, 8, 6, G, 4, 2, 2)
    for pair in range(2):
        out[:, pair, :, :6, :, :, :, pair, :] = part
    return out.reshape(256, 512)


def column_matrix():
    table = axis_table().reshape(G, G, 2, K, 2)
    out = np.zeros((G, G, 8, 2, 128), np.float32)
    for t in range(3):
        for r in range(2):
            out[:, :, 2 * t + r, :, t * K : (t + 1) * K] = table[:, :, r].transpose(1, 0, 3, 2)
    return out.reshape(2048, 256)


def order_matrix():
    out = np.zeros((G, 32, C, G), np.float32)
    for y in range(G):
        for c in range(C):
            out[y, c, c, y] = 1.0
    return out.reshape(512, CY)


def dot(a, b, contract=(1, 0)):
    return lax.dot_general(
        a, b, (((contract[0],), (contract[1],)), ((), ())), preferred_element_type=F32
    )


def pack(first, second):
    first = first.reshape(8, 8, 2 * CY)
    second = second.reshape(8, 8, 2 * CY)
    low = lax.broadcasted_iota(jnp.int32, first.shape, 1) < 4
    even = jnp.where(low, first, pltpu.roll(second, 4, 1))
    odd = jnp.where(low, pltpu.roll(first, 4, 1), second)
    return even, odd


def packed_planes(plane, depth):
    return pack(*[dot(depth, jnp.concatenate([plane(e), plane(2 + e)], 0), (1, 1)) for e in range(2)])


def send_planes(tiles, send_ref, rows):
    for parity in range(2):
        send_ref[:, parity, rows] = jnp.concatenate([tiles[0][parity], tiles[1][parity]], 1).astype(BF)


def left_rows(even, odd, e):
    low = lax.broadcasted_iota(jnp.int32, even.shape, 1) < 4
    if e == 0:
        both = jnp.where(low, even, pltpu.roll(odd, 4, 1))
    else:
        both = jnp.where(low, pltpu.roll(even, 4, 1), odd)
    return both.reshape(64, 2 * CY).T.astype(BF)


def full_planes(rows, g, e, depth, point, plane):
    left = left_rows(rows[:, 0, 8 * g : 8 * g + 8], rows[:, 1, 8 * g : 8 * g + 8], e)
    return [
        dot(
            jnp.concatenate([point, left[h * CY : (h + 1) * CY]], 1),
            jnp.concatenate([plane(2 * h + e), depth], 0),
        )
        for h in range(2)
    ]


def synthesis(rows, g, e, depth):
    even = rows[:, 0, 8 * g : 8 * g + 8]
    odd = rows[:, 1, 8 * g : 8 * g + 8]
    low = lax.broadcasted_iota(jnp.int32, even.shape, 1) < 4
    if e == 0:
        both = jnp.where(low, even, pltpu.roll(odd, 4, 1))
    else:
        both = jnp.where(low, pltpu.roll(even, 4, 1), odd)
    return dot(both.reshape(64, 2 * CY).astype(BF), depth, (0, 0))


def depth_kernel(volume_ref, depth_ref, send_ref):
    depth = depth_ref[...]
    tiles = [packed_planes(lambda k: volume_ref[:, 4 * g + k].reshape(CY, L), depth) for g in range(2)]
    send_planes(tiles, send_ref, slice(0, 16))


def row_kernel(received_ref, matrix_ref, send_ref):
    product = dot(matrix_ref[...], received_ref[...].reshape(512, 2 * CY))
    total = product[:128] + pltpu.roll(product[128:], CY, 1)
    send_ref[...] = total[:, :CY].reshape(G, 8, CY).astype(BF)


def row_back_kernel(received_ref, matrix_ref, send_ref):
    modes = received_ref[...].astype(F32).reshape(128, CY)
    zeros = jnp.zeros((128, CY), F32)
    upper = jnp.concatenate([modes, zeros], 1)
    lower = jnp.concatenate([zeros, modes], 1)
    both = jnp.concatenate([upper, lower], 0).astype(BF)
    send_ref[...] = dot(matrix_ref[...], both).reshape(G, 32, 2 * CY).astype(BF)


def column_analysis(received_ref, order_ref, column_ref):
    rows = dot(order_ref[...], received_ref[...].reshape(128, CY), (1, 1))
    lanes = jnp.concatenate([rows[32 * y : 32 * y + 32] for y in range(G)], 1)
    return dot(lanes.astype(BF), column_ref[...])


def column_synthesis(modes, order_ref, column_ref, send_ref):
    lanes = dot(modes.astype(BF), column_ref[...], (1, 1))
    rows = jnp.concatenate([lanes[:, 128 * y : 128 * y + 128] for y in range(G)], 0)
    send_ref[...] = dot(rows.astype(BF), order_ref[...], (0, 0)).reshape(G, 8, CY).astype(BF)


def weight_rows(weight_ref, i):
    spare = jnp.zeros((2 * C, 128 - 3 * K), F32)
    return jnp.concatenate([weight_ref[0, i], weight_ref[1, i], weight_ref[2, i], spare], 1)


def partner(rows):
    part = lax.broadcasted_iota(jnp.int32, rows.shape, 0) % 2
    return part == 0, jnp.where(part == 0, pltpu.roll(rows, 2 * C - 1, 0), pltpu.roll(rows, 1, 0))


def mode_factor():
    pair = lax.axis_index("gx") * 2 + lax.axis_index("gy") // 8
    return jnp.where(pair % KT == 0, 1.0, 2.0).astype(F32)


def mix_kernel(
    received_ref, order_ref, column_ref, weight_ref, send_ref, spectrum_ref, mixed_ref, parts_ref
):
    spectrum_ref[...] = column_analysis(received_ref, order_ref, column_ref)
    by_real = jnp.zeros((2 * C, 128), F32)
    by_imag = jnp.zeros((2 * C, 128), F32)
    for i in range(C):
        weight = weight_rows(weight_ref, i)
        by_real += weight * spectrum_ref[i : i + 1, :128]
        by_imag += weight * spectrum_ref[i : i + 1, 128:]
    is_real, other = partner(by_imag)
    parts_ref[...] = (by_real + jnp.where(is_real, -other, other)) * mode_factor()
    mixed_ref[...] = jnp.zeros((32, 256), F32)
    mixed_ref[:C, :128] = parts_ref[pl.ds(0, C, stride=2), :]
    mixed_ref[:C, 128:] = parts_ref[pl.ds(1, C, stride=2), :]
    column_synthesis(mixed_ref[...], order_ref, column_ref, send_ref)


def back_mix_kernel(
    received_ref, order_ref, column_ref, weight_ref, spectrum_ref,
    send_ref, gradient_ref, mixed_ref, parts_ref,
):
    mixed_ref[...] = column_analysis(received_ref, order_ref, column_ref) * mode_factor()
    parts_ref[pl.ds(0, C, stride=2), :] = mixed_ref[:C, :128]
    parts_ref[pl.ds(1, C, stride=2), :] = mixed_ref[:C, 128:]
    upstream = parts_ref[...]
    is_real, other = partner(upstream)
    turned = jnp.where(is_real, other, -other)
    mixed_ref[...] = jnp.zeros((32, 256), F32)
    for i in range(C):
        weight = weight_rows(weight_ref, i)
        mixed_ref[i : i + 1, :128] = jnp.sum(weight * upstream, 0, keepdims=True)
        mixed_ref[i : i + 1, 128:] = jnp.sum(weight * turned, 0, keepdims=True)
    column_synthesis(mixed_ref[...], order_ref, column_ref, send_ref)
    for i in range(C):
        gradient = upstream * spectrum_ref[i : i + 1, :128] + turned * spectrum_ref[i : i + 1, 128:]
        for t in range(3):
            gradient_ref[t, i] = gradient[:, t * K : (t + 1) * K]


def activation(pre):
    cumulative = 0.5 + 0.5 * lax.erf(pre * (1.0 / math.sqrt(2.0)))
    density = jnp.exp2(pre * pre * (-0.5 / math.log(2.0))) * (1.0 / math.sqrt(2.0 * math.pi))
    return cumulative, density


def spread_point(point_ref, side):
    row = lax.broadcasted_iota(jnp.int32, (CY, C), 0) // G
    repeat = jnp.where(row == lax.broadcasted_iota(jnp.int32, (CY, C), 1), 1.0, 0.0).astype(BF)
    tall = dot(repeat, point_ref[...], (1, 1 - side)).astype(BF)
    wide = dot(tall, repeat, (1, 1))
    row = lax.broadcasted_iota(jnp.int32, (CY, CY), 0) % G
    column = lax.broadcasted_iota(jnp.int32, (CY, CY), 1) % G
    return jnp.where(row == column, wide, 0.0).astype(BF)


def leave(made_ref, output_ref, left, block):
    planes = pl.ds(4 * block, 4)
    return pltpu.make_async_copy(made_ref.at[:, planes], output_ref.at[:, planes], left.at[block])


def half_rows(received_ref, half):
    return received_ref[:, :, pl.ds(pl.multiple_of(16 * half, 16), 16), :].astype(F32)


def forward_kernel(
    received_ref, volume_ref, cotangent_ref, depth_ref, point_ref, bias_ref,
    output_ref, slope_ref, send_ref, wide_ref, made_ref, left,
):
    depth = depth_ref[...]
    wide_ref[...] = spread_point(point_ref, 0)

    def step(half, carry):
        rows = half_rows(received_ref, half)
        point = wide_ref[...]
        tiles = []
        for g in range(2):
            first = 8 * half + 4 * g
            for e in range(2):
                totals = full_planes(rows, g, e, depth, point, lambda k: volume_ref[:, first + k].reshape(CY, L))
                for h in range(2):
                    x = first + 2 * h + e
                    total = totals[h]
                    for c in range(C):
                        pre = total[c * G : (c + 1) * G] + bias_ref[c]
                        cumulative, density = activation(pre)
                        made_ref[c, x] = (pre * cumulative).astype(BF)
                        slope = cotangent_ref[c, x].astype(F32) * (cumulative + pre * density)
                        slope_ref[c, x] = slope.astype(BF)
            leave(made_ref, output_ref, left, 2 * half + g).start()
            tiles.append(packed_planes(lambda k: slope_ref[:, first + k].reshape(CY, L), depth))
        send_planes(tiles, send_ref, pl.ds(pl.multiple_of(16 * half, 16), 16))
        return carry

    lax.fori_loop(0, 2, step, 0)
    for block in range(4):
        leave(made_ref, output_ref, left, block).wait()


def backward_kernel(received_ref, slope_ref, depth_ref, point_ref, output_ref, made_ref, left):
    depth = depth_ref[...]
    point = spread_point(point_ref, 1)
    for half in range(2):
        rows = half_rows(received_ref, half)
        for g in range(2):
            first = 8 * half + 4 * g
            for e in range(2):
                spectral = synthesis(rows, g, e, depth)
                for h in range(2):
                    x = first + 2 * h + e
                    total = spectral[h * CY : (h + 1) * CY] + dot(point, slope_ref[:, x].reshape(CY, L))
                    made_ref[:, x] = total.reshape(C, G, L).astype(BF)
            leave(made_ref, output_ref, left, 2 * half + g).start()
    for block in range(4):
        leave(made_ref, output_ref, left, block).wait()


SMEM = pl.BlockSpec(memory_space=pltpu.SMEM)
NEAR = pl.BlockSpec(memory_space=pltpu.VMEM)
FAR = pl.BlockSpec(memory_space=pl.ANY)
FIELD = jax.ShapeDtypeStruct((C, G, G, L), BF)
HELD = pltpu.VMEM((C, G, G, L), BF)
FOUR = pltpu.SemaphoreType.DMA((4,))
BIG = jax.ShapeDtypeStruct((8, 2, 32, 2 * CY), BF)
SMALL = jax.ShapeDtypeStruct((G, 8, CY), BF)
MODES = jax.ShapeDtypeStruct((32, 256), F32)


def call(kernel, out_shape, in_specs=None, out_specs=None, scratch=(), flops=0, moved=0, room=16, grid=()):
    extra = {}
    if in_specs is not None:
        extra = {"in_specs": in_specs, "out_specs": out_specs}
    return pl.pallas_call(
        kernel,
        out_shape=out_shape,
        grid=grid,
        scratch_shapes=scratch,
        compiler_params=pltpu.CompilerParams(vmem_limit_bytes=room * MIB),
        cost_estimate=pl.CostEstimate(flops=int(flops), bytes_accessed=moved, transcendentals=0),
        **extra,
    )


def exchange_rows(packed):
    moved = lax.all_to_all(packed.reshape(G, 32, 2 * CY), "gx", 0, 0, tiled=True)
    return moved


def exchange_columns(packed):
    return lax.all_to_all(packed, "gy", 0, 0, tiled=True)


def shards(saturation, spectral_weight, pointwise_weight, pointwise_bias, cotangent):
    depth = jnp.asarray(depth_table(), BF)
    rows = jnp.asarray(row_matrix(), BF)
    rows_back = jnp.asarray(row_matrix().T, BF)
    columns = jnp.asarray(column_matrix(), BF)
    order = jnp.asarray(order_matrix(), BF)
    weight = jnp.transpose(spectral_weight, (1, 3, 4, 0, 2)).reshape(3, C, 2 * C, K)

    depth_call = call(
        depth_kernel,
        BIG,
        [pl.BlockSpec((C, 8, G, L), lambda n: (0, n, 0, 0)), pl.BlockSpec((64, L), lambda n: (0, 0))],
        pl.BlockSpec((8, 2, 16, 2 * CY), lambda n: (0, 0, n, 0)),
        flops=170e6,
        moved=3300000,
        room=60,
        grid=(2,),
    )
    row_call = call(row_kernel, SMALL, flops=170e6, moved=1000000)
    row_back_call = call(row_back_kernel, jax.ShapeDtypeStruct((G, 32, 2 * CY), BF), flops=170e6, moved=1000000)
    mix_scratch = [pltpu.VMEM((32, 256), F32), pltpu.VMEM((2 * C, 128), F32)]
    mix_call = call(mix_kernel, (SMALL, MODES), [NEAR] * 4, (NEAR, NEAR), mix_scratch, 200e6, 2500000)
    back_mix_call = call(
        back_mix_kernel,
        (SMALL, jax.ShapeDtypeStruct((3, C, 2 * C, K), F32)),
        [NEAR] * 5,
        (NEAR, NEAR),
        mix_scratch,
        200e6,
        4000000,
    )

    received = exchange_rows(depth_call(saturation, depth))
    received = exchange_columns(row_call(received, rows))
    sent, spectrum = mix_call(received, order, columns, weight)
    received = exchange_columns(sent)
    received = exchange_rows(row_back_call(received, rows_back))
    layer_output, slope, sent = call(
        forward_kernel,
        (FIELD, FIELD, BIG),
        [NEAR] * 5 + [SMEM],
        (FAR, NEAR, NEAR),
        [pltpu.VMEM((CY, CY), BF), HELD, FOUR],
        1500e6,
        12000000,
        20,
    )(received.reshape(BIG.shape), saturation, cotangent, depth, pointwise_weight, pointwise_bias)
    received = exchange_rows(sent)
    received = exchange_columns(row_call(received, rows))
    sent, gradient = back_mix_call(received, order, columns, weight, spectrum)
    received = exchange_columns(sent)
    received = exchange_rows(row_back_call(received, rows_back))
    input_gradient = call(
        backward_kernel,
        FIELD,
        [NEAR] * 4,
        FAR,
        [HELD, FOUR],
        1300e6,
        6000000,
        16,
    )(received.reshape(BIG.shape), slope, depth, pointwise_weight)
    gradient = jnp.transpose(gradient.reshape(3, C, C, 2, K), (3, 0, 4, 1, 2))
    return layer_output, input_gradient, gradient


def solution(mesh):
    return jax.shard_map(
        shards,
        mesh=mesh,
        in_specs=(
            P(None, "gx", "gy", None),
            P(None, ("gx", "gy"), None, None, None),
            P(),
            P(),
            P(None, "gx", "gy", None),
        ),
        out_specs=(
            P(None, "gx", "gy", None),
            P(None, "gx", "gy", None),
            P(None, ("gx", "gy"), None, None, None),
        ),
        check_vma=False,
    )
```

```python
import functools
import math

import jax
import jax.numpy as jnp
import numpy as np
from jax import lax
from jax.experimental import pallas as pl
from jax.experimental.pallas import tpu as pltpu
from jax.sharding import PartitionSpec as P

C = 20
Z = 32
T_SIZE = 8
L = 256
K = 24
KZ = 8
KT = 4
M = 32
G = 16
CY = C * G
MIB = 1024 * 1024
BF = jnp.bfloat16
F32 = jnp.float32


def kept_frequency(kept_count):
    position = np.arange(kept_count)
    return np.where(position < kept_count // 2, position, position - kept_count)


def axis_table():
    product = (np.arange(L)[:, None] * kept_frequency(K)[None, :]) % L
    angle = product.astype(np.float32) * np.float32(2.0 * math.pi / L)
    cosine = np.cos(angle) * np.float32(1.0 / math.sqrt(L))
    sine = np.sin(angle) * np.float32(1.0 / math.sqrt(L))
    return np.stack([np.stack([cosine, -sine], -1), np.stack([sine, cosine], -1)], 1)


def depth_table():
    cell = np.arange(Z * T_SIZE)
    depth = ((cell // T_SIZE)[:, None] * kept_frequency(KZ)[None, :] % Z).astype(np.float32) / np.float32(Z)
    time = ((cell % T_SIZE)[:, None] * np.arange(KT)[None, :] % T_SIZE).astype(np.float32) / np.float32(T_SIZE)
    angle = (depth[:, :, None] + time[:, None, :]).reshape(Z * T_SIZE, M) * np.float32(2.0 * math.pi)
    scale = np.float32(1.0 / math.sqrt(Z * T_SIZE))
    table = np.stack([np.cos(angle) * scale, -np.sin(angle) * scale], -1)
    return table.reshape(Z * T_SIZE, 2 * M).T


def row_matrix():
    table = axis_table().reshape(G, 4, 2, 2, 2, 8, 3, 2)
    out = np.zeros((2, 2, 8, 8, G, 4, 2, 2, 2), np.float32)
    part = table.transpose(2, 5, 6, 7, 0, 1, 3, 4).reshape(2, 8, 6, G, 4, 2, 2)
    for pair in range(2):
        out[:, pair, :, :6, :, :, :, pair, :] = part
    return out.reshape(256, 512)


def column_matrix():
    table = axis_table().reshape(G, G, 2, K, 2)
    out = np.zeros((G, G, 8, 2, 128), np.float32)
    for t in range(3):
        for r in range(2):
            out[:, :, 2 * t + r, :, t * K : (t + 1) * K] = table[:, :, r].transpose(1, 0, 3, 2)
    return out.reshape(2048, 256)


def order_matrix():
    out = np.zeros((G, 32, C, G), np.float32)
    for y in range(G):
        for c in range(C):
            out[y, c, c, y] = 1.0
    return out.reshape(512, CY)


def dot(a, b, contract=(1, 0)):
    return lax.dot_general(
        a, b, (((contract[0],), (contract[1],)), ((), ())), preferred_element_type=F32
    )


def pack(first, second):
    first = first.reshape(8, 8, 2 * CY)
    second = second.reshape(8, 8, 2 * CY)
    low = lax.broadcasted_iota(jnp.int32, first.shape, 1) < 4
    even = jnp.where(low, first, pltpu.roll(second, 4, 1))
    odd = jnp.where(low, pltpu.roll(first, 4, 1), second)
    return even, odd


def packed_planes(plane, depth):
    return pack(*[dot(depth, jnp.concatenate([plane(e), plane(2 + e)], 0), (1, 1)) for e in range(2)])


def send_planes(tiles, send_ref, rows):
    for parity in range(2):
        send_ref[:, parity, rows] = jnp.concatenate([tiles[0][parity], tiles[1][parity]], 1).astype(BF)


def left_rows(even, odd, e):
    low = lax.broadcasted_iota(jnp.int32, even.shape, 1) < 4
    if e == 0:
        both = jnp.where(low, even, pltpu.roll(odd, 4, 1))
    else:
        both = jnp.where(low, pltpu.roll(even, 4, 1), odd)
    return both.reshape(64, 2 * CY).T.astype(BF)


def full_planes(rows, g, e, depth, point, plane):
    left = left_rows(rows[:, 0, 8 * g : 8 * g + 8], rows[:, 1, 8 * g : 8 * g + 8], e)
    return [
        dot(
            jnp.concatenate([point, left[h * CY : (h + 1) * CY]], 1),
            jnp.concatenate([plane(2 * h + e), depth], 0),
        )
        for h in range(2)
    ]


def synthesis(rows, g, e, depth):
    even = rows[:, 0, 8 * g : 8 * g + 8]
    odd = rows[:, 1, 8 * g : 8 * g + 8]
    low = lax.broadcasted_iota(jnp.int32, even.shape, 1) < 4
    if e == 0:
        both = jnp.where(low, even, pltpu.roll(odd, 4, 1))
    else:
        both = jnp.where(low, pltpu.roll(even, 4, 1), odd)
    return dot(both.reshape(64, 2 * CY).astype(BF), depth, (0, 0))


def depth_kernel(volume_ref, depth_ref, send_ref):
    depth = depth_ref[...]
    tiles = [packed_planes(lambda k: volume_ref[:, 4 * g + k].reshape(CY, L), depth) for g in range(2)]
    send_planes(tiles, send_ref, slice(0, 16))


def row_kernel(received_ref, matrix_ref, send_ref):
    product = dot(matrix_ref[...], received_ref[...].reshape(512, 2 * CY))
    total = product[:128] + pltpu.roll(product[128:], CY, 1)
    send_ref[...] = total[:, :CY].reshape(G, 8, CY).astype(BF)


def row_back_kernel(received_ref, matrix_ref, send_ref):
    modes = received_ref[...].astype(F32).reshape(128, CY)
    zeros = jnp.zeros((128, CY), F32)
    upper = jnp.concatenate([modes, zeros], 1)
    lower = jnp.concatenate([zeros, modes], 1)
    both = jnp.concatenate([upper, lower], 0).astype(BF)
    send_ref[...] = dot(matrix_ref[...], both).reshape(G, 32, 2 * CY).astype(BF)


def column_analysis(received_ref, order_ref, column_ref):
    rows = dot(order_ref[...], received_ref[...].reshape(128, CY), (1, 1))
    lanes = jnp.concatenate([rows[32 * y : 32 * y + 32] for y in range(G)], 1)
    return dot(lanes.astype(BF), column_ref[...])


def column_synthesis(modes, order_ref, column_ref, send_ref):
    lanes = dot(modes.astype(BF), column_ref[...], (1, 1))
    rows = jnp.concatenate([lanes[:, 128 * y : 128 * y + 128] for y in range(G)], 0)
    send_ref[...] = dot(rows.astype(BF), order_ref[...], (0, 0)).reshape(G, 8, CY).astype(BF)


def weight_rows(weight_ref, i):
    spare = jnp.zeros((2 * C, 128 - 3 * K), F32)
    return jnp.concatenate([weight_ref[0, i], weight_ref[1, i], weight_ref[2, i], spare], 1)


def partner(rows):
    part = lax.broadcasted_iota(jnp.int32, rows.shape, 0) % 2
    return part == 0, jnp.where(part == 0, pltpu.roll(rows, 2 * C - 1, 0), pltpu.roll(rows, 1, 0))


def mode_factor():
    pair = lax.axis_index("gx") * 2 + lax.axis_index("gy") // 8
    return jnp.where(pair % KT == 0, 1.0, 2.0).astype(F32)


def mix_kernel(
    received_ref, order_ref, column_ref, weight_ref, send_ref, spectrum_ref, wide_ref, mixed_ref, parts_ref
):
    spectrum_ref[...] = column_analysis(received_ref, order_ref, column_ref)
    by_real = jnp.zeros((2 * C, 128), F32)
    by_imag = jnp.zeros((2 * C, 128), F32)
    for i in range(C):
        weight = weight_rows(weight_ref, i)
        wide_ref[i] = weight
        by_real += weight * spectrum_ref[i : i + 1, :128]
        by_imag += weight * spectrum_ref[i : i + 1, 128:]
    is_real, other = partner(by_imag)
    parts_ref[...] = (by_real + jnp.where(is_real, -other, other)) * mode_factor()
    mixed_ref[...] = jnp.zeros((32, 256), F32)
    mixed_ref[:C, :128] = parts_ref[pl.ds(0, C, stride=2), :]
    mixed_ref[:C, 128:] = parts_ref[pl.ds(1, C, stride=2), :]
    column_synthesis(mixed_ref[...], order_ref, column_ref, send_ref)


def back_mix_kernel(
    received_ref, order_ref, column_ref, weight_ref, spectrum_ref,
    send_ref, gradient_ref, mixed_ref, parts_ref,
):
    mixed_ref[...] = column_analysis(received_ref, order_ref, column_ref) * mode_factor()
    parts_ref[pl.ds(0, C, stride=2), :] = mixed_ref[:C, :128]
    parts_ref[pl.ds(1, C, stride=2), :] = mixed_ref[:C, 128:]
    upstream = parts_ref[...]
    is_real, other = partner(upstream)
    turned = jnp.where(is_real, other, -other)
    mixed_ref[...] = jnp.zeros((32, 256), F32)
    for i in range(C):
        weight = weight_ref[i]
        mixed_ref[i : i + 1, :128] = jnp.sum(weight * upstream, 0, keepdims=True)
        mixed_ref[i : i + 1, 128:] = jnp.sum(weight * turned, 0, keepdims=True)
    column_synthesis(mixed_ref[...], order_ref, column_ref, send_ref)
    for i in range(C):
        gradient = upstream * spectrum_ref[i : i + 1, :128] + turned * spectrum_ref[i : i + 1, 128:]
        for t in range(3):
            gradient_ref[t, i] = gradient[:, t * K : (t + 1) * K]


def activation(pre):
    cumulative = 0.5 + 0.5 * lax.erf(pre * (1.0 / math.sqrt(2.0)))
    density = jnp.exp2(pre * pre * (-0.5 / math.log(2.0))) * (1.0 / math.sqrt(2.0 * math.pi))
    return cumulative, density


def spread_point(point_ref, side):
    row = lax.broadcasted_iota(jnp.int32, (CY, C), 0) // G
    repeat = jnp.where(row == lax.broadcasted_iota(jnp.int32, (CY, C), 1), 1.0, 0.0).astype(BF)
    tall = dot(repeat, point_ref[...], (1, 1 - side)).astype(BF)
    wide = dot(tall, repeat, (1, 1))
    row = lax.broadcasted_iota(jnp.int32, (CY, CY), 0) % G
    column = lax.broadcasted_iota(jnp.int32, (CY, CY), 1) % G
    return jnp.where(row == column, wide, 0.0).astype(BF)


def leave(made_ref, output_ref, left, block):
    planes = pl.ds(4 * block, 4)
    return pltpu.make_async_copy(made_ref.at[:, planes], output_ref.at[:, planes], left.at[block])


def half_rows(received_ref, half):
    return received_ref[:, :, pl.ds(pl.multiple_of(16 * half, 16), 16), :].astype(F32)


def forward_kernel(
    received_ref, volume_ref, cotangent_ref, depth_ref, point_ref, bias_ref,
    output_ref, slope_ref, send_ref, wide_ref, made_ref, left,
):
    depth = depth_ref[...]
    wide_ref[...] = spread_point(point_ref, 0)

    def step(half, carry):
        rows = half_rows(received_ref, half)
        point = wide_ref[...]
        tiles = []
        for g in range(2):
            first = 8 * half + 4 * g
            for e in range(2):
                totals = full_planes(rows, g, e, depth, point, lambda k: volume_ref[:, first + k].reshape(CY, L))
                for h in range(2):
                    x = first + 2 * h + e
                    total = totals[h]
                    for c in range(C):
                        pre = total[c * G : (c + 1) * G] + bias_ref[c]
                        cumulative, density = activation(pre)
                        made_ref[c, x] = (pre * cumulative).astype(BF)
                        slope = cotangent_ref[c, x].astype(F32) * (cumulative + pre * density)
                        slope_ref[c, x] = slope.astype(BF)
            leave(made_ref, output_ref, left, 2 * half + g).start()
            tiles.append(packed_planes(lambda k: slope_ref[:, first + k].reshape(CY, L), depth))
        send_planes(tiles, send_ref, pl.ds(pl.multiple_of(16 * half, 16), 16))
        return carry

    lax.fori_loop(0, 2, step, 0)
    for block in range(4):
        leave(made_ref, output_ref, left, block).wait()


def backward_kernel(received_ref, slope_ref, depth_ref, point_ref, output_ref, made_ref, left):
    depth = depth_ref[...]
    point = spread_point(point_ref, 1)
    for half in range(2):
        rows = half_rows(received_ref, half)
        for g in range(2):
            first = 8 * half + 4 * g
            for e in range(2):
                spectral = synthesis(rows, g, e, depth)
                for h in range(2):
                    x = first + 2 * h + e
                    total = spectral[h * CY : (h + 1) * CY] + dot(point, slope_ref[:, x].reshape(CY, L))
                    made_ref[:, x] = total.reshape(C, G, L).astype(BF)
            leave(made_ref, output_ref, left, 2 * half + g).start()
    for block in range(4):
        leave(made_ref, output_ref, left, block).wait()


SMEM = pl.BlockSpec(memory_space=pltpu.SMEM)
NEAR = pl.BlockSpec(memory_space=pltpu.VMEM)
FAR = pl.BlockSpec(memory_space=pl.ANY)
FIELD = jax.ShapeDtypeStruct((C, G, G, L), BF)
HELD = pltpu.VMEM((C, G, G, L), BF)
FOUR = pltpu.SemaphoreType.DMA((4,))
BIG = jax.ShapeDtypeStruct((8, 2, 32, 2 * CY), BF)
SMALL = jax.ShapeDtypeStruct((G, 8, CY), BF)
MODES = jax.ShapeDtypeStruct((32, 256), F32)


def call(kernel, out_shape, in_specs=None, out_specs=None, scratch=(), flops=0, moved=0, room=16, grid=()):
    extra = {}
    if in_specs is not None:
        extra = {"in_specs": in_specs, "out_specs": out_specs}
    return pl.pallas_call(
        kernel,
        out_shape=out_shape,
        grid=grid,
        scratch_shapes=scratch,
        compiler_params=pltpu.CompilerParams(vmem_limit_bytes=room * MIB),
        cost_estimate=pl.CostEstimate(flops=int(flops), bytes_accessed=moved, transcendentals=0),
        **extra,
    )


def exchange_rows(packed):
    moved = lax.all_to_all(packed.reshape(G, 32, 2 * CY), "gx", 0, 0, tiled=True)
    return moved


def exchange_columns(packed):
    return lax.all_to_all(packed, "gy", 0, 0, tiled=True)


def shards(saturation, spectral_weight, pointwise_weight, pointwise_bias, cotangent):
    depth = jnp.asarray(depth_table(), BF)
    rows = jnp.asarray(row_matrix(), BF)
    rows_back = jnp.asarray(row_matrix().T, BF)
    columns = jnp.asarray(column_matrix(), BF)
    order = jnp.asarray(order_matrix(), BF)
    weight = jnp.transpose(spectral_weight, (1, 3, 4, 0, 2)).reshape(3, C, 2 * C, K)

    depth_call = call(
        depth_kernel,
        BIG,
        [pl.BlockSpec((C, 8, G, L), lambda n: (0, n, 0, 0)), pl.BlockSpec((64, L), lambda n: (0, 0))],
        pl.BlockSpec((8, 2, 16, 2 * CY), lambda n: (0, 0, n, 0)),
        flops=170e6,
        moved=3300000,
        room=60,
        grid=(2,),
    )
    row_call = call(row_kernel, SMALL, flops=170e6, moved=1000000)
    row_back_call = call(row_back_kernel, jax.ShapeDtypeStruct((G, 32, 2 * CY), BF), flops=170e6, moved=1000000)
    mix_scratch = [pltpu.VMEM((32, 256), F32), pltpu.VMEM((2 * C, 128), F32)]
    wide = jax.ShapeDtypeStruct((C, 2 * C, 128), F32)
    mix_call = call(mix_kernel, (SMALL, MODES, wide), [NEAR] * 4, (NEAR,) * 3, mix_scratch, 200e6, 2500000)
    back_mix_call = call(
        back_mix_kernel,
        (SMALL, jax.ShapeDtypeStruct((3, C, 2 * C, K), F32)),
        [NEAR] * 5,
        (NEAR, NEAR),
        mix_scratch,
        200e6,
        4000000,
    )

    received = exchange_rows(depth_call(saturation, depth))
    received = exchange_columns(row_call(received, rows))
    sent, spectrum, weight = mix_call(received, order, columns, weight)
    received = exchange_columns(sent)
    received = exchange_rows(row_back_call(received, rows_back))
    layer_output, slope, sent = call(
        forward_kernel,
        (FIELD, FIELD, BIG),
        [NEAR] * 5 + [SMEM],
        (FAR, NEAR, NEAR),
        [pltpu.VMEM((CY, CY), BF), HELD, FOUR],
        1500e6,
        12000000,
        20,
    )(received.reshape(BIG.shape), saturation, cotangent, depth, pointwise_weight, pointwise_bias)
    received = exchange_rows(sent)
    received = exchange_columns(row_call(received, rows))
    sent, gradient = back_mix_call(received, order, columns, weight, spectrum)
    received = exchange_columns(sent)
    received = exchange_rows(row_back_call(received, rows_back))
    input_gradient = call(
        backward_kernel,
        FIELD,
        [NEAR] * 4,
        FAR,
        [HELD, FOUR],
        1300e6,
        6000000,
        16,
    )(received.reshape(BIG.shape), slope, depth, pointwise_weight)
    gradient = jnp.transpose(gradient.reshape(3, C, C, 2, K), (3, 0, 4, 1, 2))
    return layer_output, input_gradient, gradient


def solution(mesh):
    return jax.shard_map(
        shards,
        mesh=mesh,
        in_specs=(
            P(None, "gx", "gy", None),
            P(None, ("gx", "gy"), None, None, None),
            P(),
            P(),
            P(None, "gx", "gy", None),
        ),
        out_specs=(
            P(None, "gx", "gy", None),
            P(None, "gx", "gy", None),
            P(None, ("gx", "gy"), None, None, None),
        ),
        check_vma=False,
    )
```
